768 devices in a mesh: section: 3 (over z_hi), dp: 256 (over y, z_lo, x, core).
Axes of the slice: x: 4, y: 8, z: 12 (z_hi: 3, z_lo: 4; z = z_hi * 4 + z_lo), core: 2. Of those that a mesh axis runs over, the one named last changes fastest.
Arguments:
- hidden: bfloat16 [768, 256, 3584], P(('section', 'dp')), may hold values from -1000 to 1000, as said below
- lengths: int32 [768], P(('section', 'dp')), may hold values from 64 to 256, as said below
- pair_perm: int32 [384], replicated, may hold values from 0 to 383, as said below
- norm_gain: bfloat16 [3584], replicated, may hold values from 0.099609375 to 1.8984375
- projection: bfloat16 [3584, 1024], replicated, may hold values from -0.09375 to 0.09375
Outputs:
- hidden_grad: bfloat16 [768, 256, 3584], P(('section', 'dp'))
- loss: float32 [], replicated
The draws below stay inside these ranges and needn't reach their ends.
Inputs may be any that keep to these rules, and one draw needn't show every extreme that they name: hidden rows of the encoder, finite. `lengths`: every sequence holds at least 64 valid tokens, and some sequence fills all 256 positions. `pair_perm`: a permutation: each docstring is paired with exactly one code.
All inputs are finite; a program needn't handle non-finite values.
Results may differ from the reference program's by a relative error of at most 0.008.
Values may be sent and summed in bfloat16 or wider, within the bound.
A program may use at most 32 MiB of HBM per device.

```python
import jax
import jax.numpy as jnp
from jax import lax

D = 3584
E = 1024
LEN = 256
SEQS = 768
PAIRS = 384


def shared_perm(key):
    return jax.random.permutation(jax.random.fold_in(key, 11), PAIRS).astype(jnp.int32)


def draw_pair_perm(key, part):
    return shared_perm(key)


def draw_hidden(key, part):
    perm = shared_perm(key)
    inverse = jnp.zeros((PAIRS,), jnp.int32).at[perm].set(jnp.arange(PAIRS, dtype=jnp.int32))
    pair_of = jnp.concatenate([jnp.arange(PAIRS, dtype=jnp.int32), inverse]).astype(jnp.int32)
    cluster_of = (pair_of // 4).astype(jnp.int32)
    keys = jax.random.split(jax.random.fold_in(key, 5), 10)
    pair_dirs = jax.random.normal(keys[0], (PAIRS, D), jnp.float32)
    cluster_dirs = jax.random.normal(keys[1], (PAIRS, D), jnp.float32)
    batch_dir = jax.random.normal(keys[2], (1, D), jnp.float32)
    own_dirs = jax.random.normal(keys[3], (SEQS, D), jnp.float32)
    seq_pos = jnp.arange(SEQS, dtype=jnp.float32) / SEQS
    pair_weight = jax.random.uniform(keys[4], (PAIRS,), jnp.float32, 0.18, 0.3)
    cluster_weight = jax.random.uniform(keys[5], (PAIRS,), jnp.float32, 0.15, 0.3)
    common_weight = jax.random.uniform(keys[6], (SEQS,), jnp.float32, 0.0, 1.0) * (0.2 + 0.4 * seq_pos)
    base = jax.random.normal(keys[7], (SEQS, LEN, D), jnp.float32)
    component = pair_weight[pair_of][:, None] * pair_dirs[pair_of]
    component = component + cluster_weight[cluster_of][:, None] * cluster_dirs[cluster_of]
    component = component + common_weight[:, None] * batch_dir + 0.5 * own_dirs
    row_scales = jnp.exp(jax.random.uniform(keys[8], (SEQS, LEN, 1), jnp.float32, 0.0, 2.3))
    chan_scales = jnp.exp(jax.random.uniform(keys[9], (1, 1, D), jnp.float32, 0.0, 2.3))
    mixed = jnp.clip(base + component[:, None, :], -8.0, 8.0)
    return (mixed * row_scales * chan_scales).astype(jnp.bfloat16)


def draw_lengths(key, part):
    key_len, key_spot = jax.random.split(jax.random.fold_in(key, 7))
    shortest = max(1, LEN // 4)
    drawn_lengths = jax.random.randint(key_len, (SEQS,), shortest, LEN + 1, dtype=jnp.int32)
    longest_at = jax.random.randint(key_spot, (), 0, SEQS, dtype=jnp.int32)
    return jnp.where(jnp.arange(SEQS, dtype=jnp.int32) == longest_at, LEN, drawn_lengths).astype(jnp.int32)


def gaussian(own_key, shape, spread, bound, kind=jnp.bfloat16):
    return jnp.clip(spread * jax.random.normal(own_key, shape, jnp.float32), -bound, bound).astype(kind)


def setup_inputs(seed: int = 0) -> dict:
    key_list = jax.random.split(jax.random.key(seed), 6)
    return {
        "hidden": draw_hidden(jax.random.fold_in(key_list[5], 71), 0),
        "lengths": draw_lengths(jax.random.fold_in(key_list[5], 71), 0),
        "pair_perm": draw_pair_perm(jax.random.fold_in(key_list[5], 71), 0),
        "norm_gain": jnp.clip(1.0 + 0.18 * jax.random.normal(key_list[3], (D,), jnp.float32), 0.099609375, 1.8984375).astype(jnp.bfloat16),
        "projection": gaussian(key_list[4], (D, E), D ** -0.5, 0.09375),
    }


inv_temp = 20.0
loss_scale = 1024.0
norm_eps = 1e-06

def partners(pair_perm):
    pair_count = pair_perm.shape[0]
    order_ids = jnp.arange(pair_count, dtype=jnp.int32)
    inverse = jnp.zeros((pair_count,), jnp.int32).at[pair_perm].set(order_ids)
    return jnp.concatenate([pair_perm + pair_count, inverse]).astype(jnp.int32)

def pool_one(seq_rows, length, gain_f):
    values = seq_rows.astype(jnp.float32)
    inv_rms = lax.rsqrt(lax.optimization_barrier(jnp.mean(values * values, axis=1)) + norm_eps)
    share = (jnp.arange(seq_rows.shape[0], dtype=jnp.int32) < length).astype(jnp.float32) / length.astype(jnp.float32)
    return lax.optimization_barrier(jnp.sum((share * inv_rms)[:, None] * values, axis=0)) * gain_f

def back_one(seq_rows, length, scaled):
    values = seq_rows.astype(jnp.float32)
    inv_rms = lax.rsqrt(lax.optimization_barrier(jnp.mean(values * values, axis=1)) + norm_eps)
    share = (jnp.arange(seq_rows.shape[0], dtype=jnp.int32) < length).astype(jnp.float32) / length.astype(jnp.float32)
    dot_rows = lax.optimization_barrier(jnp.sum(values * scaled[None, :], axis=1))
    result = share[:, None] * (inv_rms[:, None] * scaled[None, :] - values * (inv_rms ** 3 * dot_rows / seq_rows.shape[1])[:, None])
    return result.astype(jnp.bfloat16)

def reference(hidden, lengths, pair_perm, norm_gain, projection):
    gain_f = norm_gain.astype(jnp.float32)
    seq_count = hidden.shape[0]
    pair_count = seq_count // 2
    pooled = lax.map(lambda item: pool_one(item[0], item[1], gain_f), (hidden, lengths)).astype(jnp.bfloat16)
    raw_emb = jnp.dot(pooled, projection, preferred_element_type=jnp.float32)
    magnitude = jnp.sqrt(lax.optimization_barrier(jnp.sum(raw_emb * raw_emb, axis=1, keepdims=True)) + norm_eps)
    unit = raw_emb / magnitude
    emb = unit.astype(jnp.bfloat16)
    codes = emb[:pair_count]
    docs = emb[pair_count:]
    scores = inv_temp * jnp.dot(codes, docs.T, preferred_element_type=jnp.float32)
    exp_scores = jnp.exp(scores)
    code_totals = lax.optimization_barrier(jnp.sum(exp_scores, axis=1))
    doc_totals = lax.optimization_barrier(jnp.sum(exp_scores, axis=0))
    columns = jnp.arange(pair_count, dtype=jnp.int32)
    target = (columns[None, :] == pair_perm[:, None]).astype(jnp.float32)
    loss = (jnp.sum(jnp.log(code_totals)) + jnp.sum(jnp.log(doc_totals)) - 2.0 * jnp.sum(target * scores)) / seq_count
    factors = exp_scores / code_totals[:, None] + exp_scores / doc_totals[None, :] - 2.0 * target
    factor = loss_scale * inv_temp
    grad_codes = factor * jnp.dot(factors, docs.astype(jnp.float32), precision=lax.Precision.HIGHEST)
    grad_docs = factor * jnp.dot(factors.T, codes.astype(jnp.float32), precision=lax.Precision.HIGHEST)
    demb = jnp.concatenate([grad_codes, grad_docs], axis=0)
    projected = lax.optimization_barrier(jnp.sum(unit * demb, axis=1, keepdims=True))
    grad_raw = ((demb - unit * projected) / magnitude).astype(jnp.bfloat16)
    grad_pooled = jnp.dot(grad_raw, projection.T, preferred_element_type=jnp.float32)
    scaled = grad_pooled * gain_f[None, :]
    hidden_grad = lax.map(lambda item: back_one(item[0], item[1], item[2]), (hidden, lengths, scaled))
    return (hidden_grad, loss)
```

```python
import functools

import jax
import jax.numpy as jnp
from jax import lax
from jax.experimental import pallas as pl
from jax.experimental.pallas import tpu as pltpu
from jax.sharding import PartitionSpec as P

MESH = pl.DeviceIdType.MESH
ANY = pl.BlockSpec(memory_space=pl.ANY)
SMEM = pl.BlockSpec(memory_space=pltpu.SMEM)
VMEM = pl.BlockSpec(memory_space=pltpu.VMEM)
bf16, f32 = jnp.bfloat16, jnp.float32

INV_TEMP = 20.0
LOSS_SCALE = 1024.0
EPS = 1e-06

NX, NY, NZ = 4, 8, 12
ROWS = 64
PROJ = 512

XC = [(x, 0, 0, c) for x in range(NX) for c in range(2) if (x, c) != (0, 0)]
FAR = [(0, y, z, 0) for z in (0, 4, 8) for y in (0, 2, 4, 6) if (y, z) != (0, 0)]
ZNEAR = [(0, 0, 1, 0), (0, 0, -1, 0), (0, 0, 2, 0), (0, 0, -2, 0)]
YNEAR = [(0, 1, 0, 0), (0, -1, 0, 0)]
PEERS = XC + FAR + ZNEAR + YNEAR
N_COPIES = len(XC) + len(FAR) + len(ZNEAR) + 4 * len(YNEAR) + 8


def contract_last(a, b):
    return lax.dot_general(a, b, (((1,), (1,)), ((), ())), preferred_element_type=f32)


def split3(v):
    hi = v.astype(bf16)
    rest = v - hi.astype(f32)
    mid = rest.astype(bf16)
    return hi, mid, (rest - mid.astype(f32)).astype(bf16)


def stack3(row):
    hi, mid, lo = split3(jnp.broadcast_to(row, (16, row.shape[1])))
    i = lax.broadcasted_iota(jnp.int32, hi.shape, 0)
    zero = jnp.zeros_like(hi)
    return jnp.where(i == 0, hi, jnp.where(i == 1, mid, jnp.where(i == 2, lo, zero)))


def main_kernel(
    hidden, lengths, perm_s, perm_v, gain_h, proj_h,
    g_out, coef_out, loss_out,
    x_v, proj, proj_t, gain_v, packets, emb, target, pooled_v,
    in_sem, send_sem, recv_sem,
):
    z_hi = lax.axis_index("section")
    dp = lax.axis_index("dp")
    core = dp % 2
    x = (dp // 2) % NX
    z_lo = (dp // (2 * NX)) % 4
    y = dp // (8 * NX)
    z = z_hi * 4 + z_lo
    y_far, y_par = y // 2, y % 2

    def device(d):
        xx = (x + d[0]) % NX
        yy = (y + d[1] + NY) % NY
        zz = (z + d[2] + NZ) % NZ
        cc = (core + d[3]) % 2
        return (zz // 4, ((yy * 4 + zz % 4) * NX + xx) * 2 + cc)

    barrier = pltpu.get_barrier_semaphore()

    width = x_v.shape[1]
    length_rows = x_v.shape[0]
    n_x, n_p = length_rows // ROWS, width // PROJ
    loads = [
        pltpu.make_async_copy(
            hidden.at[0, pl.ds(i * ROWS, ROWS)], x_v.at[pl.ds(i * ROWS, ROWS)], in_sem.at[i]
        )
        for i in range(n_x)
    ]
    loads.append(pltpu.make_async_copy(gain_h, gain_v, in_sem.at[n_x]))
    loads += [
        pltpu.make_async_copy(
            proj_h.at[pl.ds(i * PROJ, PROJ)], proj.at[pl.ds(i * PROJ, PROJ)], in_sem.at[n_x + 1 + i]
        )
        for i in range(n_p)
    ]
    for load in loads:
        load.start()
    for d in PEERS:
        pl.semaphore_signal(barrier, inc=1, device_id=device(d), device_id_type=MESH)

    length = lengths[0]
    inv_len = 1.0 / jnp.full((1, 1), length, jnp.int32).astype(f32)
    pooled = jnp.zeros((1, width), f32)
    for i in range(n_x):
        loads[i].wait()
        rows = pl.ds(i * ROWS, ROWS)
        sums = jnp.zeros((ROWS, 128), f32)
        for k in range(width // 128):
            v = x_v[rows, k * 128 : (k + 1) * 128].astype(f32)
            sums = sums + v * v
        inv_rms = lax.rsqrt(jnp.sum(sums, axis=1, keepdims=True) / width + EPS)
        position = lax.broadcasted_iota(jnp.int32, (ROWS, 1), 0) + i * ROWS
        share = jnp.where(position < length, inv_len, 0.0)
        weight = share * inv_rms
        cubed = weight * inv_rms * inv_rms / width
        lane = lax.broadcasted_iota(jnp.int32, (ROWS, 128), 1)
        coef_out[rows, :] = jnp.where(lane == 0, weight, cubed)
        weight_row = jnp.broadcast_to(weight, (ROWS, 128)).T[0:1, :]
        parts = jnp.dot(stack3(weight_row), x_v[rows, :], preferred_element_type=f32)
        pooled = pooled + (parts[0:1] + (parts[1:2] + parts[2:3]))
    loads[n_x].wait()
    gain = gain_v[...].astype(f32).reshape(1, width)
    pooled_v[...] = jnp.broadcast_to(pooled * gain, (16, width)).astype(bf16)

    raw = jnp.zeros((16, proj.shape[1]), f32)
    for i in range(n_p):
        loads[n_x + 1 + i].wait()
        cut = slice(i * PROJ, (i + 1) * PROJ)
        raw = raw + jnp.dot(pooled_v[:, cut], proj[cut, :], preferred_element_type=f32)
    raw = raw[0:8]
    magnitude = jnp.sqrt(jnp.sum(raw * raw, axis=1, keepdims=True) + EPS)
    unit = raw / magnitude
    own = unit.astype(bf16)
    sub = lax.broadcasted_iota(jnp.int32, (8, 128), 0)
    packet = jnp.zeros((8, 128), f32)
    for k in range(8):
        packet = jnp.where(sub == k, own[:, k * 128 : (k + 1) * 128].astype(f32), packet)
    mine = x * 2 + core
    my_rows = pl.ds(pl.multiple_of(mine * 8, 8), 8)
    packets[my_rows, :] = packet

    count = [0]

    def copy(src, dst, d):
        k = count[0]
        count[0] += 1
        out = pltpu.make_async_remote_copy(
            src_ref=src, dst_ref=dst, send_sem=send_sem.at[k], recv_sem=recv_sem.at[k],
            device_id=device(d), device_id_type=MESH,
        )
        out.start()
        sent.append(out)
        return out

    sent = []
    half = pl.multiple_of(core * 512, 512)
    all_half = pl.ds(half, 512)
    quarters = [pl.ds(half, 256), pl.ds(pl.multiple_of(half + 256, 256), 256)]

    pl.semaphore_wait(barrier, len(PEERS))
    phase1 = [copy(packets.at[my_rows], packets.at[my_rows], d) for d in XC]
    for c in phase1:
        c.wait_recv()
    block = emb.at[z_hi, y_far, y_par, z_lo]
    for k in range(8):
        @pl.when(k // 4 == core)
        def _(k=k):
            part = packets[pl.ds(k, 8, stride=8), :]
            block[:, k * 128 : (k + 1) * 128] = part.astype(bf16)
    cut = emb.at[z_hi, y_far, y_par, z_lo, :, all_half]
    phase2 = [copy(cut, cut, d) for d in FAR]

    def transpose(i, _):
        at = pl.ds(pl.multiple_of(i * 256, 256), 256)
        proj_t[:, at] = proj[at, :].T
        return 0

    lax.fori_loop(0, width // 256, transpose, 0)
    pairs = target.shape[0]
    perm_row = perm_v[...].astype(f32).reshape(1, pairs)
    perm_col = jnp.broadcast_to(perm_row, (128, pairs)).T[:, 0:1]
    column = lax.broadcasted_iota(jnp.int32, (pairs, pairs), 1).astype(f32)
    target[...] = jnp.where(column == perm_col, 1.0, 0.0)

    for c in phase2:
        c.wait_recv()

    def znear(k):
        cols = all_half if k < 2 else quarters[k - 2]
        part = emb.at[:, :, y_par, z_lo, :, cols]
        return copy(part, part, ZNEAR[k])

    def ynear(zl):
        out = []
        for k in range(2):
            part = emb.at[:, :, y_par, zl, :, quarters[k]]
            out.append(copy(part, part, YNEAR[k]))
        return out

    def sibling(par, zl):
        part = emb.at[:, :, par, zl, :, all_half]
        return copy(part, part, (0, 0, 0, 1))

    phase3 = [znear(k) for k in range(4)]
    classes = [z_lo, (z_lo + 3) % 4, (z_lo + 1) % 4, (z_lo + 2) % 4]
    phase4, phase5 = [ynear(classes[0])], [sibling(y_par, classes[0])]
    for k in (1, 2, 3):
        for c in phase3[k - 1 : k] if k < 3 else phase3[2:]:
            c.wait_recv()
        phase4.append(ynear(classes[k]))
        phase5.append(sibling(y_par, classes[k]))
    for k in range(4):
        for c in phase4[k]:
            c.wait_recv()
        phase5.append(sibling(1 - y_par, classes[k]))
    for c in phase5:
        c.wait_recv()
    for c in sent:
        c.wait_send()

    everyone = emb[...].reshape(2 * pairs, emb.shape[-1])
    codes, docs = everyone[:pairs], everyone[pairs:]
    scores = INV_TEMP * contract_last(codes, docs)
    exps = jnp.exp(scores)
    code_totals = jnp.sum(exps, axis=1, keepdims=True)
    doc_totals = jnp.sum(exps, axis=0, keepdims=True)
    log_sum = jnp.sum(jnp.log(doc_totals)) + jnp.sum(jnp.log(code_totals))
    loss_out[0, 0] = (log_sum - 2.0 * jnp.sum(target[...] * scores)) / (2 * pairs)
    code_row = jnp.broadcast_to(code_totals, (pairs, 128)).T[0:1, :]

    me = z_hi * (pairs * 2 // 3) + dp
    is_code = me < pairs
    other_totals = jnp.where(is_code, doc_totals, code_row)
    other_blocks = jnp.where(is_code, pairs // 8, 0)
    flat = emb.reshape(2 * pairs // 8, 8, emb.shape[-1])
    others = flat[pl.ds(other_blocks, pairs // 8)].reshape(pairs, emb.shape[-1])
    own_exps = jnp.exp(INV_TEMP * contract_last(own, others)[0:1, :])
    own_total = jnp.sum(own_exps, axis=1, keepdims=True)
    columns = lax.broadcasted_iota(jnp.int32, (1, pairs), 1)
    code_id = jnp.where(is_code, me, 0)
    doc_id = jnp.where(is_code, 0, me - pairs)
    code_hit = columns == jnp.full((1, 1), perm_s[code_id], jnp.int32)
    doc_hit = perm_row == jnp.full((1, 1), doc_id, jnp.int32).astype(f32)
    hit = jnp.where(is_code, jnp.where(code_hit, 1.0, 0.0), jnp.where(doc_hit, 1.0, 0.0))
    factors = own_exps / own_total + own_exps / other_totals - 2.0 * hit
    terms = jnp.dot(stack3(factors), others, preferred_element_type=f32)
    demb = (LOSS_SCALE * INV_TEMP) * (terms[0:1] + (terms[1:2] + terms[2:3]))
    unit_row = unit[0:1]
    projected = jnp.sum(unit_row * demb, axis=1, keepdims=True)
    grad_raw = (demb - unit_row * projected) / magnitude[0:1]
    grad_rows = jnp.broadcast_to(grad_raw, (16, grad_raw.shape[1])).astype(bf16)
    grad_pooled = jnp.dot(grad_rows, proj_t[...], preferred_element_type=f32)
    g_out[...] = grad_pooled[0:1] * gain


def out_kernel(hidden, g, coef, out):
    rows = hidden[0]
    terms = contract_last(rows, stack3(g[...]))
    dots = terms[:, 0:1] + (terms[:, 1:2] + terms[:, 2:3])
    weight = coef[:, 0:1]
    cubed = coef[:, 1:2] * dots
    out[0] = (weight * g[...] - rows.astype(f32) * cubed).astype(bf16)


def body(hidden, lengths, pair_perm, norm_gain, projection):
    _, length_rows, width = hidden.shape
    embed = projection.shape[1]
    pairs = pair_perm.shape[0]
    g, coef, loss = pl.pallas_call(
        main_kernel,
        out_shape=(
            jax.ShapeDtypeStruct((1, width), f32),
            jax.ShapeDtypeStruct((length_rows, 128), f32),
            jax.ShapeDtypeStruct((1, 1), f32),
        ),
        in_specs=[ANY, SMEM, SMEM, VMEM, ANY, ANY],
        out_specs=(VMEM, VMEM, SMEM),
        scratch_shapes=[
            pltpu.VMEM((length_rows, width), bf16),
            pltpu.VMEM((width, embed), bf16),
            pltpu.VMEM((embed, width), bf16),
            pltpu.VMEM((width,), bf16),
            pltpu.VMEM((64, 128), f32),
            pltpu.VMEM((3, 4, 2, 4, 8, embed), bf16),
            pltpu.VMEM((pairs, pairs), f32),
            pltpu.VMEM((16, width), bf16),
            pltpu.SemaphoreType.DMA((length_rows // ROWS + 1 + width // PROJ,)),
            pltpu.SemaphoreType.DMA((N_COPIES,)),
            pltpu.SemaphoreType.DMA((N_COPIES,)),
        ],
        compiler_params=pltpu.CompilerParams(
            collective_id=0, has_side_effects=True, vmem_limit_bytes=48 << 20
        ),
        name="main",
    )(hidden, lengths, pair_perm, pair_perm, norm_gain, projection)
    grad = pl.pallas_call(
        out_kernel,
        grid=(length_rows // ROWS,),
        out_shape=jax.ShapeDtypeStruct(hidden.shape, bf16),
        in_specs=[
            pl.BlockSpec((1, ROWS, width), lambda i: (0, i, 0)),
            pl.BlockSpec((1, width), lambda i: (0, 0)),
            pl.BlockSpec((ROWS, 128), lambda i: (i, 0)),
        ],
        out_specs=pl.BlockSpec((1, ROWS, width), lambda i: (0, i, 0)),
        compiler_params=pltpu.CompilerParams(vmem_limit_bytes=32 << 20),
        name="hidden_grad",
    )(hidden, g, coef)
    return grad, loss.reshape(())


def solution(mesh):
    in_specs = (P(("section", "dp"), None, None), P(("section", "dp")), P(), P(), P())
    out_specs = (P(("section", "dp"), None, None), P())
    return jax.shard_map(body, mesh=mesh, in_specs=in_specs, out_specs=out_specs, check_vma=False)
```

```python
import functools

import jax
import jax.numpy as jnp
from jax import lax
from jax.experimental import pallas as pl
from jax.experimental.pallas import tpu as pltpu
from jax.sharding import PartitionSpec as P

MESH = pl.DeviceIdType.MESH
HBM = pl.BlockSpec(memory_space=pltpu.HBM)
SMEM = pl.BlockSpec(memory_space=pltpu.SMEM)
VMEM = pl.BlockSpec(memory_space=pltpu.VMEM)
bf16, f32 = jnp.bfloat16, jnp.float32

INV_TEMP = 20.0
LOSS_SCALE = 1024.0
EPS = 1e-06

NX, NY, NZ = 4, 8, 12
ROWS = 64
PROJ = 512

XC = [(x, 0, 0, c) for x in range(NX) for c in range(2) if (x, c) != (0, 0)]
FAR = [(0, 4, 4), (0, 4, 8), (0, 2, 4), (0, 2, 8), (0, 6, 4), (0, 6, 8), (0, 4, 0)]
FAR += [(0, 0, 4), (0, 0, 8), (0, 2, 0), (0, 6, 0)]
FIRST, SECOND, WHOLE = (0, 2), (2, 2), (0, 4)
MID = [
    ((0, 1), [((1, 0, 1), WHOLE)]),
    ((0, -1), [((3, 0, -1), WHOLE)]),
    ((1, 1), [((3, 1, 1), FIRST), ((3, -1, 1), SECOND)]),
    ((1, -1), [((1, 1, -1), FIRST), ((1, -1, -1), SECOND)]),
    ((1, 0), [((2, 1, 0), FIRST), ((2, -1, 0), SECOND)]),
    ((1, 2), [((0, 1, 2), FIRST), ((0, -1, -2), SECOND)]),
    ((0, 2), [((2, 0, 2), FIRST), ((2, 0, -2), SECOND)]),
]
LAST = [
    ((1, 0, 0), FIRST), ((3, 0, 0), FIRST), ((0, 0, 1), SECOND),
    ((0, 0, -1), SECOND), ((0, 1, 0), FIRST), ((0, -1, 0), SECOND),
]
SIBLING = (0, 0, 0, 1)
OTHER_CHIPS = FAR + [d for _, copies in MID for d, _ in copies] + [d for d, _ in LAST]
PEERS = sorted({(x, y % NY, z % NZ, c) for x, y, z, c in XC + [(*d, 0) for d in OTHER_CHIPS]})
AT_FAR = len(XC)
AT_MID = AT_FAR + len(FAR)
AT_LAST = AT_MID + 2 * len(MID)
AT_SIB = AT_LAST + 8 * len(LAST)
N_COPIES = AT_SIB + 8


def contract_last(a, b):
    return lax.dot_general(a, b, (((1,), (1,)), ((), ())), preferred_element_type=f32)


def split3(v):
    hi = v.astype(bf16)
    rest = v - hi.astype(f32)
    mid = rest.astype(bf16)
    return hi, mid, (rest - mid.astype(f32)).astype(bf16)


def stack3(row):
    hi, mid, lo = split3(jnp.broadcast_to(row, (16, row.shape[1])))
    i = lax.broadcasted_iota(jnp.int32, hi.shape, 0)
    zero = jnp.zeros_like(hi)
    return jnp.where(i == 0, hi, jnp.where(i == 1, mid, jnp.where(i == 2, lo, zero)))


def main_kernel(
    hidden, lengths_h, perm_h, gain_h, proj_h,
    g_out, coef_out, loss_out,
    lengths, perm_s, perm_v, x_v, proj, proj_t, gain_v, gain_f, packets, emb, target, pooled_v, xg_proj,
    in_sem, small_sem, send_sem, recv_sem,
):
    z_hi = lax.axis_index("section")
    dp = lax.axis_index("dp")
    core = dp % 2
    x = (dp // 2) % NX
    z_lo = (dp // (2 * NX)) % 4
    y = dp // (8 * NX)
    z = z_hi * 4 + z_lo
    y_far, y_par = y // 2, y % 2

    def device(d):
        xx = (x + d[0]) % NX
        yy = (y + d[1] + NY) % NY
        zz = (z + d[2] + NZ) % NZ
        cc = (core + d[3]) % 2 if len(d) == 4 else core
        return (zz // 4, ((yy * 4 + zz % 4) * NX + xx) * 2 + cc)

    barrier = pltpu.get_barrier_semaphore()

    width = x_v.shape[1]
    length_rows = x_v.shape[0]
    n_x, n_p = length_rows // ROWS, width // PROJ
    loads = [
        pltpu.make_async_copy(
            hidden.at[0, pl.ds(i * ROWS, ROWS)], x_v.at[pl.ds(i * ROWS, ROWS)], in_sem.at[i]
        )
        for i in range(n_x)
    ]
    loads += [
        pltpu.make_async_copy(
            proj_h.at[pl.ds(i * PROJ, PROJ)], proj.at[pl.ds(i * PROJ, PROJ)], in_sem.at[n_x + i]
        )
        for i in range(n_p)
    ]
    small = [
        pltpu.make_async_copy(src, dst, small_sem.at[i])
        for i, (src, dst) in enumerate(
            ((lengths_h, lengths), (gain_h, gain_v), (perm_h, perm_s), (perm_h, perm_v))
        )
    ]
    for load in small + loads:
        load.start()
    for d in PEERS:
        pl.semaphore_signal(barrier, inc=1, device_id=device(d), device_id_type=MESH)

    small[0].wait()
    length = lengths[0]
    inv_len = 1.0 / jnp.full((1, 1), length, jnp.int32).astype(f32)
    pooled = jnp.zeros((1, width), f32)
    for i in range(n_x):
        loads[i].wait()
        rows = pl.ds(i * ROWS, ROWS)
        sums = jnp.zeros((ROWS, 128), f32)
        for k in range(width // 128):
            v = x_v[rows, k * 128 : (k + 1) * 128].astype(f32)
            sums = sums + v * v
        inv_rms = lax.rsqrt(jnp.sum(sums, axis=1, keepdims=True) / width + EPS)
        position = lax.broadcasted_iota(jnp.int32, (ROWS, 1), 0) + i * ROWS
        share = jnp.where(position < length, inv_len, 0.0)
        weight = share * inv_rms
        cubed = weight * inv_rms * inv_rms / width
        lane = lax.broadcasted_iota(jnp.int32, (ROWS, 128), 1)
        coef_out[rows, :] = jnp.where(lane == 0, weight, cubed)
        weight_row = jnp.broadcast_to(weight, (ROWS, 128)).T[0:1, :]
        parts = jnp.dot(stack3(weight_row), x_v[rows, :], preferred_element_type=f32)
        pooled = pooled + (parts[0:1] + (parts[1:2] + parts[2:3]))
    small[1].wait()
    gain_f[...] = gain_v[...].astype(f32).reshape(1, width)
    gain = gain_f[...]
    pooled_v[...] = jnp.broadcast_to(pooled * gain, (16, width)).astype(bf16)

    raw = jnp.zeros((16, proj.shape[1]), f32)
    for i in range(n_p):
        loads[n_x + i].wait()
        cut = slice(i * PROJ, (i + 1) * PROJ)
        raw = raw + jnp.dot(pooled_v[:, cut], proj[cut, :], preferred_element_type=f32)
    raw = raw[0:8]
    magnitude = jnp.sqrt(jnp.sum(raw * raw, axis=1, keepdims=True) + EPS)
    unit = raw / magnitude
    own = unit.astype(bf16)
    sub = lax.broadcasted_iota(jnp.int32, (8, 128), 0)
    packet = jnp.zeros((8, 128), f32)
    for k in range(8):
        packet = jnp.where(sub == k, own[:, k * 128 : (k + 1) * 128].astype(f32), packet)
    mine = x * 2 + core
    my_rows = pl.ds(pl.multiple_of(mine * 8, 8), 8)
    packets[my_rows, :] = packet

    for c in small[2:]:
        c.wait()
    pairs = target.shape[0]
    perm_row = perm_v[...].astype(f32).reshape(1, pairs)

    def prepare():
        def transpose(i, _):
            at = pl.ds(pl.multiple_of(i * 256, 256), 256)
            proj_t[:, at] = proj[at, :].T
            return 0

        lax.fori_loop(0, width // 256, transpose, 0)
        perm_col = jnp.broadcast_to(perm_row, (128, pairs)).T[:, 0:1]
        column = lax.broadcasted_iota(jnp.int32, (pairs, pairs), 1).astype(f32)
        target[...] = jnp.where(column == perm_col, 1.0, 0.0)
        xg_proj[...] = jnp.zeros_like(xg_proj)

        def gained(i, _):
            at = pl.ds(pl.multiple_of(i * PROJ, PROJ), PROJ)
            xg = x_v[:, at].astype(f32) * gain_f[:, at]
            high = xg.astype(bf16)
            low = (xg - high.astype(f32)).astype(bf16)
            both = jnp.dot(
                jnp.concatenate([high, low], axis=0), proj[at, :], preferred_element_type=f32
            )
            xg_proj[...] += both[:length_rows] + both[length_rows:]
            return 0

        lax.fori_loop(0, n_p, gained, 0)

    pl.when(z_hi == 0)(prepare)

    sent = []

    def copy(k, ref, d):
        out = pltpu.make_async_remote_copy(
            src_ref=ref, dst_ref=ref, send_sem=send_sem.at[k], recv_sem=recv_sem.at[k],
            device_id=device(d), device_id_type=MESH,
        )
        out.start()
        sent.append(out)
        return out

    def tile(q):
        return pl.ds(pl.multiple_of(core * 512 + (q % 4) * 128, 128), 128)

    pl.semaphore_wait(barrier, len(PEERS))
    arriving = [copy(i, packets.at[my_rows], d) for i, d in enumerate(XC)]
    for c in arriving:
        c.wait_recv()
    block = emb.at[z_hi, y_far, y_par, z_lo]
    for k in range(8):
        @pl.when(k == core * 4 + x)
        def _(k=k):
            part = packets[pl.ds(k, 8, stride=8), :]
            block[:, k * 128 : (k + 1) * 128] = part.astype(bf16)

    cut = emb.at[z_hi, y_far, y_par, z_lo, :, tile(x)]
    arriving = [copy(AT_FAR + i, cut, d) for i, d in enumerate(FAR)]
    for c in arriving:
        c.wait_recv()

    near = []
    for i, (_, copies) in enumerate(MID):
        near.append([
            copy(AT_MID + 2 * i + j, emb.at[:, pl.ds(*part), y_par, z_lo, :, tile(x)], d)
            for j, (d, part) in enumerate(copies)
        ])

    held = x - 2 * y - z + 32
    classes = [(y_par, z_lo)]
    classes += [((y_par + dy) % 2, (z_lo - dz + 4) % 4) for (dy, dz), _ in MID]
    neighbours = []
    for i, (par, lo) in enumerate(classes):
        for c in near[i - 1] if i else ():
            c.wait_recv()
        base = AT_LAST + len(LAST) * (4 * par + lo)
        cols = tile(held + 2 * par + lo)
        neighbours.append([
            copy(base + j, emb.at[:, pl.ds(*part), par, lo, :, cols], d)
            for j, (d, part) in enumerate(LAST)
        ])
    half = pl.ds(pl.multiple_of(core * 512, 512), 512)
    arriving = []
    for i, (par, lo) in enumerate(classes):
        for c in neighbours[i]:
            c.wait_recv()
        arriving.append(copy(AT_SIB + 4 * par + lo, emb.at[:, :, par, lo, :, half], SIBLING))
    pl.when(z_hi != 0)(prepare)
    for c in arriving:
        c.wait_recv()

    everyone = emb[...].reshape(2 * pairs, emb.shape[-1])
    codes, docs = everyone[:pairs], everyone[pairs:]
    scores = INV_TEMP * contract_last(codes, docs)
    exps = jnp.exp(scores)
    code_totals = jnp.sum(exps, axis=1, keepdims=True)
    doc_totals = jnp.sum(exps, axis=0, keepdims=True)
    log_sum = jnp.sum(jnp.log(doc_totals)) + jnp.sum(jnp.log(code_totals))
    loss_out[0, 0] = (log_sum - 2.0 * jnp.sum(target[...] * scores)) / (2 * pairs)
    code_row = jnp.broadcast_to(code_totals, (pairs, 128)).T[0:1, :]

    me = z_hi * (pairs * 2 // 3) + dp
    is_code = me < pairs
    other_totals = jnp.where(is_code, doc_totals, code_row)
    other_blocks = jnp.where(is_code, pairs // 8, 0)
    flat = emb.reshape(2 * pairs // 8, 8, emb.shape[-1])
    others = flat[pl.ds(other_blocks, pairs // 8)].reshape(pairs, emb.shape[-1])
    own_exps = jnp.exp(INV_TEMP * contract_last(own, others)[0:1, :])
    own_total = jnp.sum(own_exps, axis=1, keepdims=True)
    columns = lax.broadcasted_iota(jnp.int32, (1, pairs), 1)
    code_id = jnp.where(is_code, me, 0)
    doc_id = jnp.where(is_code, 0, me - pairs)
    code_hit = columns == jnp.full((1, 1), perm_s[code_id], jnp.int32)
    doc_hit = perm_row == jnp.full((1, 1), doc_id, jnp.int32).astype(f32)
    hit = jnp.where(is_code, jnp.where(code_hit, 1.0, 0.0), jnp.where(doc_hit, 1.0, 0.0))
    factors = own_exps / own_total + own_exps / other_totals - 2.0 * hit
    terms = jnp.dot(stack3(factors), others, preferred_element_type=f32)
    demb = (LOSS_SCALE * INV_TEMP) * (terms[0:1] + (terms[1:2] + terms[2:3]))
    unit_row = unit[0:1]
    projected = jnp.sum(unit_row * demb, axis=1, keepdims=True)
    grad_raw = (demb - unit_row * projected) / magnitude[0:1]
    grad_rows = jnp.broadcast_to(grad_raw, (16, grad_raw.shape[1])).astype(bf16)
    grad_pooled = jnp.dot(grad_rows, proj_t[...], preferred_element_type=f32)
    g_out[...] = grad_pooled[0:1] * gain_f[...]
    dots = jnp.sum(xg_proj[...] * grad_rows[0:1].astype(f32), axis=1, keepdims=True)
    lane = lax.broadcasted_iota(jnp.int32, coef_out.shape, 1)
    coef_out[...] = jnp.where(lane == 1, coef_out[...] * dots, coef_out[...])
    for c in sent:
        c.wait_send()


def out_kernel(hidden, g, coef, out):
    out[0] = (coef[:, 0:1] * g[...] - hidden[0].astype(f32) * coef[:, 1:2]).astype(bf16)


def body(hidden, lengths, pair_perm, norm_gain, projection):
    _, length_rows, width = hidden.shape
    embed = projection.shape[1]
    pairs = pair_perm.shape[0]
    g, coef, loss = pl.pallas_call(
        main_kernel,
        out_shape=(
            jax.ShapeDtypeStruct((1, width), f32),
            jax.ShapeDtypeStruct((length_rows, 128), f32),
            jax.ShapeDtypeStruct((1, 1), f32),
        ),
        in_specs=[HBM] * 5,
        out_specs=(VMEM, VMEM, SMEM),
        scratch_shapes=[
            pltpu.SMEM(lengths.shape, jnp.int32),
            pltpu.SMEM(pair_perm.shape, jnp.int32),
            pltpu.VMEM(pair_perm.shape, jnp.int32),
            pltpu.VMEM((length_rows, width), bf16),
            pltpu.VMEM((width, embed), bf16),
            pltpu.VMEM((embed, width), bf16),
            pltpu.VMEM((width,), bf16),
            pltpu.VMEM((1, width), f32),
            pltpu.VMEM((64, 128), f32),
            pltpu.VMEM((3, 4, 2, 4, 8, embed), bf16),
            pltpu.VMEM((pairs, pairs), f32),
            pltpu.VMEM((16, width), bf16),
            pltpu.VMEM((length_rows, embed), f32),
            pltpu.SemaphoreType.DMA((length_rows // ROWS + width // PROJ,)),
            pltpu.SemaphoreType.DMA((4,)),
            pltpu.SemaphoreType.DMA((N_COPIES,)),
            pltpu.SemaphoreType.DMA((N_COPIES,)),
        ],
        compiler_params=pltpu.CompilerParams(
            collective_id=0, has_side_effects=True, vmem_limit_bytes=60 << 20
        ),
        name="main",
    )(hidden, lengths, pair_perm, norm_gain, projection)
    grad = pl.pallas_call(
        out_kernel,
        grid=(length_rows // ROWS,),
        out_shape=jax.ShapeDtypeStruct(hidden.shape, bf16),
        in_specs=[
            pl.BlockSpec((1, ROWS, width), lambda i: (0, i, 0)),
            pl.BlockSpec((1, width), lambda i: (0, 0)),
            pl.BlockSpec((ROWS, 128), lambda i: (i, 0)),
        ],
        out_specs=pl.BlockSpec((1, ROWS, width), lambda i: (0, i, 0)),
        compiler_params=pltpu.CompilerParams(vmem_limit_bytes=60 << 20),
        name="hidden_grad",
    )(hidden, g, coef)
    return grad, loss.reshape(())


def solution(mesh):
    in_specs = (P(("section", "dp"), None, None), P(("section", "dp")), P(), P(), P())
    out_specs = (P(("section", "dp"), None, None), P())
    return jax.shard_map(body, mesh=mesh, in_specs=in_specs, out_specs=out_specs, check_vma=False)
```

```python
import functools

import jax
import jax.numpy as jnp
from jax import lax
from jax.experimental import pallas as pl
from jax.experimental.pallas import tpu as pltpu
from jax.sharding import PartitionSpec as P

MESH = pl.DeviceIdType.MESH
HBM = pl.BlockSpec(memory_space=pltpu.HBM)
SMEM = pl.BlockSpec(memory_space=pltpu.SMEM)
VMEM = pl.BlockSpec(memory_space=pltpu.VMEM)
bf16, f32 = jnp.bfloat16, jnp.float32

INV_TEMP = 20.0
LOSS_SCALE = 1024.0
EPS = 1e-06

NX, NY, NZ = 4, 8, 12
ROWS = 64
OUT_ROWS = 32
PROJ = 512

XC = [(x, 0, 0, c) for x in range(NX) for c in range(2) if (x, c) != (0, 0)]
FAR = [(0, 4, 4), (0, 4, 8), (0, 2, 4), (0, 2, 8), (0, 6, 4), (0, 6, 8), (0, 4, 0)]
FAR += [(0, 0, 4), (0, 0, 8), (0, 2, 0), (0, 6, 0)]
FIRST, SECOND, WHOLE = (0, 2), (2, 2), (0, 4)
MID = [
    ((0, 1), [((1, 0, 1), WHOLE)]),
    ((0, -1), [((3, 0, -1), WHOLE)]),
    ((1, 1), [((3, 1, 1), FIRST), ((3, -1, 1), SECOND)]),
    ((1, -1), [((1, 1, -1), FIRST), ((1, -1, -1), SECOND)]),
    ((1, 0), [((2, 1, 0), FIRST), ((2, -1, 0), SECOND)]),
    ((1, 2), [((0, 1, 2), FIRST), ((0, -1, -2), SECOND)]),
    ((0, 2), [((2, 0, 2), FIRST), ((2, 0, -2), SECOND)]),
]
LAST = [
    ((1, 0, 0), FIRST), ((3, 0, 0), FIRST), ((0, 0, 1), SECOND),
    ((0, 0, -1), SECOND), ((0, 1, 0), FIRST), ((0, -1, 0), SECOND),
]
SIBLING = (0, 0, 0, 1)
OTHER_CHIPS = FAR + [d for _, copies in MID for d, _ in copies] + [d for d, _ in LAST]
PEERS = sorted({(x, y % NY, z % NZ, c) for x, y, z, c in XC + [(*d, 0) for d in OTHER_CHIPS]})
AT_FAR = len(XC)
AT_MID = AT_FAR + len(FAR)
AT_LAST = AT_MID + 2 * len(MID)
AT_SIB = AT_LAST + 8 * len(LAST)
N_COPIES = AT_SIB + 8


def contract_last(a, b):
    return lax.dot_general(a, b, (((1,), (1,)), ((), ())), preferred_element_type=f32)


def split3(v):
    hi = v.astype(bf16)
    rest = v - hi.astype(f32)
    mid = rest.astype(bf16)
    return hi, mid, (rest - mid.astype(f32)).astype(bf16)


def stack3(row):
    hi, mid, lo = split3(jnp.broadcast_to(row, (16, row.shape[1])))
    i = lax.broadcasted_iota(jnp.int32, hi.shape, 0)
    zero = jnp.zeros_like(hi)
    return jnp.where(i == 0, hi, jnp.where(i == 1, mid, jnp.where(i == 2, lo, zero)))


def main_kernel(
    hidden, lengths_h, perm_h, gain_h, proj_h,
    g_out, coef_out, loss_out,
    lengths, perm_s, perm_v, x_v, proj, proj_t, gain_v, gain_f, packets, emb, target, pooled_v, xg_proj,
    in_sem, small_sem, send_sem, recv_sem,
):
    z_hi = lax.axis_index("section")
    dp = lax.axis_index("dp")
    core = dp % 2
    x = (dp // 2) % NX
    z_lo = (dp // (2 * NX)) % 4
    y = dp // (8 * NX)
    z = z_hi * 4 + z_lo
    y_far, y_par = y // 2, y % 2

    def device(d):
        xx = (x + d[0]) % NX
        yy = (y + d[1] + NY) % NY
        zz = (z + d[2] + NZ) % NZ
        cc = (core + d[3]) % 2 if len(d) == 4 else core
        return (zz // 4, ((yy * 4 + zz % 4) * NX + xx) * 2 + cc)

    barrier = pltpu.get_barrier_semaphore()

    width = x_v.shape[1]
    length_rows = x_v.shape[0]
    n_x, n_p = length_rows // ROWS, width // PROJ
    loads = [
        pltpu.make_async_copy(
            hidden.at[0, pl.ds(i * ROWS, ROWS)], x_v.at[pl.ds(i * ROWS, ROWS)], in_sem.at[i]
        )
        for i in range(n_x)
    ]
    loads += [
        pltpu.make_async_copy(
            proj_h.at[pl.ds(i * PROJ, PROJ)], proj.at[pl.ds(i * PROJ, PROJ)], in_sem.at[n_x + i]
        )
        for i in range(n_p)
    ]
    small = [
        pltpu.make_async_copy(src, dst, small_sem.at[i])
        for i, (src, dst) in enumerate(
            ((lengths_h, lengths), (gain_h, gain_v), (perm_h, perm_s), (perm_h, perm_v))
        )
    ]
    for load in small + loads:
        load.start()
    for d in PEERS:
        pl.semaphore_signal(barrier, inc=1, device_id=device(d), device_id_type=MESH)

    small[0].wait()
    length = lengths[0]
    inv_len = 1.0 / jnp.full((1, 1), length, jnp.int32).astype(f32)
    pooled = jnp.zeros((1, width), f32)
    for i in range(n_x):
        loads[i].wait()
        rows = pl.ds(i * ROWS, ROWS)
        sums = jnp.zeros((ROWS, 128), f32)
        for k in range(width // 128):
            v = x_v[rows, k * 128 : (k + 1) * 128].astype(f32)
            sums = sums + v * v
        inv_rms = lax.rsqrt(jnp.sum(sums, axis=1, keepdims=True) / width + EPS)
        position = lax.broadcasted_iota(jnp.int32, (ROWS, 1), 0) + i * ROWS
        share = jnp.where(position < length, inv_len, 0.0)
        weight = share * inv_rms
        cubed = weight * inv_rms * inv_rms / width
        lane = lax.broadcasted_iota(jnp.int32, (ROWS, 128), 1)
        coef_out[rows, :] = jnp.where(lane == 0, weight, cubed)
        weight_row = jnp.broadcast_to(weight, (ROWS, 128)).T[0:1, :]
        parts = jnp.dot(stack3(weight_row), x_v[rows, :], preferred_element_type=f32)
        pooled = pooled + (parts[0:1] + (parts[1:2] + parts[2:3]))
    small[1].wait()
    gain_f[...] = gain_v[...].astype(f32).reshape(1, width)
    gain = gain_f[...]
    pooled_v[...] = jnp.broadcast_to(pooled * gain, (16, width)).astype(bf16)

    raw = jnp.zeros((16, proj.shape[1]), f32)
    for i in range(n_p):
        loads[n_x + i].wait()
        cut = slice(i * PROJ, (i + 1) * PROJ)
        raw = raw + jnp.dot(pooled_v[:, cut], proj[cut, :], preferred_element_type=f32)
    raw = raw[0:8]
    magnitude = jnp.sqrt(jnp.sum(raw * raw, axis=1, keepdims=True) + EPS)
    unit = raw / magnitude
    own = unit.astype(bf16)
    sub = lax.broadcasted_iota(jnp.int32, (8, 128), 0)
    packet = jnp.zeros((8, 128), f32)
    for k in range(8):
        packet = jnp.where(sub == k, own[:, k * 128 : (k + 1) * 128].astype(f32), packet)
    mine = x * 2 + core
    my_rows = pl.ds(pl.multiple_of(mine * 8, 8), 8)
    packets[my_rows, :] = packet

    for c in small[2:]:
        c.wait()
    pairs = target.shape[0]
    perm_row = perm_v[...].astype(f32).reshape(1, pairs)

    def prepare():
        def transpose(i, _):
            at = pl.ds(pl.multiple_of(i * 256, 256), 256)
            proj_t[:, at] = proj[at, :].T
            return 0

        lax.fori_loop(0, width // 256, transpose, 0)
        perm_col = jnp.broadcast_to(perm_row, (128, pairs)).T[:, 0:1]
        column = lax.broadcasted_iota(jnp.int32, (pairs, pairs), 1).astype(f32)
        target[...] = jnp.where(column == perm_col, 1.0, 0.0)
        xg_proj[...] = jnp.zeros_like(xg_proj)

        def gained(i, _):
            at = pl.ds(pl.multiple_of(i * PROJ, PROJ), PROJ)
            xg = x_v[:, at].astype(f32) * gain_f[:, at]
            high = xg.astype(bf16)
            low = (xg - high.astype(f32)).astype(bf16)
            both = jnp.dot(
                jnp.concatenate([high, low], axis=0), proj[at, :], preferred_element_type=f32
            )
            xg_proj[...] += both[:length_rows] + both[length_rows:]
            return 0

        lax.fori_loop(0, n_p, gained, 0)

    pl.when(z_hi == 0)(prepare)

    def copy(k, ref, d):
        out = pltpu.make_async_remote_copy(
            src_ref=ref, dst_ref=ref, send_sem=send_sem.at[k], recv_sem=recv_sem.at[k],
            device_id=device(d), device_id_type=MESH,
        )
        out.start()
        return out

    def sent(copies):
        for c in copies:
            c.wait_send()

    def tile(q):
        return pl.ds(pl.multiple_of(core * 512 + (q % 4) * 128, 128), 128)

    pl.semaphore_wait(barrier, len(PEERS))
    rows_in = [copy(i, packets.at[my_rows], d) for i, d in enumerate(XC)]
    for c in rows_in:
        c.wait_recv()
    block = emb.at[z_hi, y_far, y_par, z_lo]
    for k in range(8):
        @pl.when(k == core * 4 + x)
        def _(k=k):
            part = packets[pl.ds(k, 8, stride=8), :]
            block[:, k * 128 : (k + 1) * 128] = part.astype(bf16)

    cut = emb.at[z_hi, y_far, y_par, z_lo, :, tile(x)]
    far_in = [copy(AT_FAR + i, cut, d) for i, d in enumerate(FAR)]
    sent(rows_in)
    for c in far_in:
        c.wait_recv()

    near = []
    for i, (_, copies) in enumerate(MID):
        near.append([
            copy(AT_MID + 2 * i + j, emb.at[:, pl.ds(*part), y_par, z_lo, :, tile(x)], d)
            for j, (d, part) in enumerate(copies)
        ])

    held = x - 2 * y - z + 32
    classes = [(y_par, z_lo)]
    classes += [((y_par + dy) % 2, (z_lo - dz + 4) % 4) for (dy, dz), _ in MID]
    neighbours = []
    for i, (par, lo) in enumerate(classes):
        for c in near[i - 1] if i else ():
            c.wait_recv()
        base = AT_LAST + len(LAST) * (4 * par + lo)
        cols = tile(held + 2 * par + lo)
        neighbours.append([
            copy(base + j, emb.at[:, pl.ds(*part), par, lo, :, cols], d)
            for j, (d, part) in enumerate(LAST)
        ])
        if i == 0:
            sent(far_in)
    for copies in near:
        sent(copies)
    half = pl.ds(pl.multiple_of(core * 512, 512), 512)
    arriving = []
    for i, (par, lo) in enumerate(classes):
        for c in neighbours[i]:
            c.wait_recv()
        arriving.append(copy(AT_SIB + 4 * par + lo, emb.at[:, :, par, lo, :, half], SIBLING))
    for copies in neighbours:
        sent(copies)
    pl.when(z_hi != 0)(prepare)
    for c in arriving:
        c.wait_recv()

    everyone = emb[...].reshape(2 * pairs, emb.shape[-1])
    codes, docs = everyone[:pairs], everyone[pairs:]
    scores = INV_TEMP * contract_last(codes, docs)
    exps = jnp.exp(scores)
    code_totals = jnp.sum(exps, axis=1, keepdims=True)
    doc_totals = jnp.sum(exps, axis=0, keepdims=True)
    log_sum = jnp.sum(jnp.log(doc_totals)) + jnp.sum(jnp.log(code_totals))
    loss_out[0, 0] = (log_sum - 2.0 * jnp.sum(target[...] * scores)) / (2 * pairs)
    code_row = jnp.broadcast_to(code_totals, (pairs, 128)).T[0:1, :]

    me = z_hi * (pairs * 2 // 3) + dp
    is_code = me < pairs
    other_totals = jnp.where(is_code, doc_totals, code_row)
    other_blocks = jnp.where(is_code, pairs // 8, 0)
    flat = emb.reshape(2 * pairs // 8, 8, emb.shape[-1])
    others = flat[pl.ds(other_blocks, pairs // 8)].reshape(pairs, emb.shape[-1])
    own_exps = jnp.exp(INV_TEMP * contract_last(own, others)[0:1, :])
    own_total = jnp.sum(own_exps, axis=1, keepdims=True)
    columns = lax.broadcasted_iota(jnp.int32, (1, pairs), 1)
    code_id = jnp.where(is_code, me, 0)
    doc_id = jnp.where(is_code, 0, me - pairs)
    code_hit = columns == jnp.full((1, 1), perm_s[code_id], jnp.int32)
    doc_hit = perm_row == jnp.full((1, 1), doc_id, jnp.int32).astype(f32)
    hit = jnp.where(is_code, jnp.where(code_hit, 1.0, 0.0), jnp.where(doc_hit, 1.0, 0.0))
    factors = own_exps / own_total + own_exps / other_totals - 2.0 * hit
    terms = jnp.dot(stack3(factors), others, preferred_element_type=f32)
    demb = (LOSS_SCALE * INV_TEMP) * (terms[0:1] + (terms[1:2] + terms[2:3]))
    unit_row = unit[0:1]
    projected = jnp.sum(unit_row * demb, axis=1, keepdims=True)
    grad_raw = (demb - unit_row * projected) / magnitude[0:1]
    grad_rows = jnp.broadcast_to(grad_raw, (16, grad_raw.shape[1])).astype(bf16)
    grad_pooled = jnp.dot(grad_rows, proj_t[...], preferred_element_type=f32)
    g_out[...] = grad_pooled[0:1] * gain_f[...]
    dots = jnp.sum(xg_proj[...] * grad_rows[0:1].astype(f32), axis=1, keepdims=True)
    lane = lax.broadcasted_iota(jnp.int32, coef_out.shape, 1)
    coef_out[...] = jnp.where(lane == 1, coef_out[...] * dots, coef_out[...])
    for c in arriving:
        c.wait_send()


def out_kernel(hidden, g_h, coef_h, out, x_v, g, coef, o_v, in_sem, out_sem):
    n, rows = x_v.shape[0] // OUT_ROWS, [pl.ds(i, OUT_ROWS) for i in range(0, x_v.shape[0], OUT_ROWS)]
    small = [
        pltpu.make_async_copy(g_h, g, in_sem.at[n]),
        pltpu.make_async_copy(coef_h, coef, in_sem.at[n + 1]),
    ]
    loads = [pltpu.make_async_copy(hidden.at[0, r], x_v.at[r], in_sem.at[i]) for i, r in enumerate(rows)]
    stores = [pltpu.make_async_copy(o_v.at[r], out.at[0, r], out_sem.at[i]) for i, r in enumerate(rows)]
    for c in small + loads:
        c.start()
    for c in small:
        c.wait()
    for r, load, store in zip(rows, loads, stores):
        load.wait()
        grad = coef[r, 0:1] * g[...] - x_v[r, :].astype(f32) * coef[r, 1:2]
        o_v[r, :] = grad.astype(bf16)
        store.start()
    for store in stores:
        store.wait()


def body(hidden, lengths, pair_perm, norm_gain, projection):
    _, length_rows, width = hidden.shape
    embed = projection.shape[1]
    pairs = pair_perm.shape[0]
    g, coef, loss = pl.pallas_call(
        main_kernel,
        out_shape=(
            jax.ShapeDtypeStruct((1, width), f32),
            jax.ShapeDtypeStruct((length_rows, 128), f32),
            jax.ShapeDtypeStruct((1, 1), f32),
        ),
        in_specs=[HBM] * 5,
        out_specs=(VMEM, VMEM, SMEM),
        scratch_shapes=[
            pltpu.SMEM(lengths.shape, jnp.int32),
            pltpu.SMEM(pair_perm.shape, jnp.int32),
            pltpu.VMEM(pair_perm.shape, jnp.int32),
            pltpu.VMEM((length_rows, width), bf16),
            pltpu.VMEM((width, embed), bf16),
            pltpu.VMEM((embed, width), bf16),
            pltpu.VMEM((width,), bf16),
            pltpu.VMEM((1, width), f32),
            pltpu.VMEM((64, 128), f32),
            pltpu.VMEM((3, 4, 2, 4, 8, embed), bf16),
            pltpu.VMEM((pairs, pairs), f32),
            pltpu.VMEM((16, width), bf16),
            pltpu.VMEM((length_rows, embed), f32),
            pltpu.SemaphoreType.DMA((length_rows // ROWS + width // PROJ,)),
            pltpu.SemaphoreType.DMA((4,)),
            pltpu.SemaphoreType.DMA((N_COPIES,)),
            pltpu.SemaphoreType.DMA((N_COPIES,)),
        ],
        compiler_params=pltpu.CompilerParams(
            collective_id=0, has_side_effects=True, vmem_limit_bytes=60 << 20
        ),
        name="main",
    )(hidden, lengths, pair_perm, norm_gain, projection)
    n_out = length_rows // OUT_ROWS
    grad = pl.pallas_call(
        out_kernel,
        out_shape=jax.ShapeDtypeStruct(hidden.shape, bf16),
        in_specs=[HBM] * 3,
        out_specs=HBM,
        scratch_shapes=[
            pltpu.VMEM((length_rows, width), bf16),
            pltpu.VMEM((1, width), f32),
            pltpu.VMEM((length_rows, 128), f32),
            pltpu.VMEM((length_rows, width), bf16),
            pltpu.SemaphoreType.DMA((n_out + 2,)),
            pltpu.SemaphoreType.DMA((n_out,)),
        ],
        compiler_params=pltpu.CompilerParams(vmem_limit_bytes=60 << 20),
        name="hidden_grad",
    )(hidden, g, coef)
    return grad, loss.reshape(())


def solution(mesh):
    in_specs = (P(("section", "dp"), None, None), P(("section", "dp")), P(), P(), P())
    out_specs = (P(("section", "dp"), None, None), P())
    return jax.shard_map(body, mesh=mesh, in_specs=in_specs, out_specs=out_specs, check_vma=False)
```

```python
import functools

import jax
import jax.numpy as jnp
from jax import lax
from jax.experimental import pallas as pl
from jax.experimental.pallas import tpu as pltpu
from jax.sharding import PartitionSpec as P

MESH = pl.DeviceIdType.MESH
HBM = pl.BlockSpec(memory_space=pltpu.HBM)
SMEM = pl.BlockSpec(memory_space=pltpu.SMEM)
VMEM = pl.BlockSpec(memory_space=pltpu.VMEM)
bf16, f32 = jnp.bfloat16, jnp.float32

INV_TEMP = 20.0
LOSS_SCALE = 1024.0
EPS = 1e-06

NX, NY, NZ = 4, 8, 12
ROWS = 64
OUT_ROWS = 32
PROJ = 512

XC = [(x, 0, 0, c) for x in range(NX) for c in range(2) if (x, c) != (0, 0)]
FAR = [(0, 4, 4), (0, 4, 8), (0, 2, 4), (0, 2, 8), (0, 6, 4), (0, 6, 8), (0, 4, 0)]
FAR += [(0, 0, 4), (0, 0, 8), (0, 2, 0), (0, 6, 0)]
FIRST, SECOND, WHOLE = (0, 2), (2, 2), (0, 4)
MID = [
    ((0, 1), [((1, 0, 1), WHOLE)]),
    ((0, -1), [((3, 0, -1), WHOLE)]),
    ((1, 1), [((3, 1, 1), FIRST), ((3, -1, 1), SECOND)]),
    ((1, -1), [((1, 1, -1), FIRST), ((1, -1, -1), SECOND)]),
    ((1, 0), [((2, 1, 0), FIRST), ((2, -1, 0), SECOND)]),
    ((1, 2), [((0, 1, 2), FIRST), ((0, -1, -2), SECOND)]),
    ((0, 2), [((2, 0, 2), FIRST), ((2, 0, -2), SECOND)]),
]
LAST = [
    ((1, 0, 0), FIRST), ((3, 0, 0), FIRST), ((0, 0, 1), SECOND),
    ((0, 0, -1), SECOND), ((0, 1, 0), FIRST), ((0, -1, 0), SECOND),
]
SIBLING = (0, 0, 0, 1)
OTHER_CHIPS = FAR + [d for _, copies in MID for d, _ in copies] + [d for d, _ in LAST]
PEERS = sorted({(x, y % NY, z % NZ, c) for x, y, z, c in XC + [(*d, 0) for d in OTHER_CHIPS]})
AT_FAR = len(XC)
AT_MID = AT_FAR + len(FAR)
AT_LAST = AT_MID + 2 * len(MID)
AT_SIB = AT_LAST + 8 * len(LAST)
N_COPIES = AT_SIB + 8


def contract_last(a, b):
    return lax.dot_general(a, b, (((1,), (1,)), ((), ())), preferred_element_type=f32)


def split3(v):
    hi = v.astype(bf16)
    rest = v - hi.astype(f32)
    mid = rest.astype(bf16)
    return hi, mid, (rest - mid.astype(f32)).astype(bf16)


def stack3(row):
    hi, mid, lo = split3(jnp.broadcast_to(row, (16, row.shape[1])))
    i = lax.broadcasted_iota(jnp.int32, hi.shape, 0)
    zero = jnp.zeros_like(hi)
    return jnp.where(i == 0, hi, jnp.where(i == 1, mid, jnp.where(i == 2, lo, zero)))


def main_kernel(
    hidden, lengths_h, perm_h, gain_h, proj_h,
    g_out, coef_out, loss_out,
    lengths, perm_s, perm_v, x_v, proj, proj_t, gain_v, gain_f, pieces, rows8, emb, target, score_v, pooled_v, xg_proj,
    in_sem, small_sem, send_sem, recv_sem,
):
    z_hi = lax.axis_index("section")
    dp = lax.axis_index("dp")
    core = dp % 2
    x = (dp // 2) % NX
    z_lo = (dp // (2 * NX)) % 4
    y = dp // (8 * NX)
    z = z_hi * 4 + z_lo
    y_far, y_par = y // 2, y % 2

    def device(d):
        xx = (x + d[0]) % NX
        yy = (y + d[1] + NY) % NY
        zz = (z + d[2] + NZ) % NZ
        cc = (core + d[3]) % 2 if len(d) == 4 else core
        return (zz // 4, ((yy * 4 + zz % 4) * NX + xx) * 2 + cc)

    barrier = pltpu.get_barrier_semaphore()

    width = x_v.shape[1]
    length_rows = x_v.shape[0]
    n_x, n_p = length_rows // ROWS, width // PROJ
    loads = [
        pltpu.make_async_copy(
            hidden.at[0, pl.ds(i * ROWS, ROWS)], x_v.at[pl.ds(i * ROWS, ROWS)], in_sem.at[i]
        )
        for i in range(n_x)
    ]
    loads += [
        pltpu.make_async_copy(
            proj_h.at[pl.ds(i * PROJ, PROJ)], proj.at[pl.ds(i * PROJ, PROJ)], in_sem.at[n_x + i]
        )
        for i in range(n_p)
    ]
    small = [
        pltpu.make_async_copy(src, dst, small_sem.at[i])
        for i, (src, dst) in enumerate(
            ((lengths_h, lengths), (gain_h, gain_v), (perm_h, perm_s), (perm_h, perm_v))
        )
    ]
    for load in small + loads:
        load.start()
    for d in PEERS:
        pl.semaphore_signal(barrier, inc=1, device_id=device(d), device_id_type=MESH)

    small[0].wait()
    length = lengths[0]
    inv_len = 1.0 / jnp.full((1, 1), length, jnp.int32).astype(f32)
    pooled = jnp.zeros((1, width), f32)
    for i in range(n_x):
        loads[i].wait()
        rows = pl.ds(i * ROWS, ROWS)
        sums = jnp.zeros((ROWS, 128), f32)
        for k in range(width // 128):
            v = x_v[rows, k * 128 : (k + 1) * 128].astype(f32)
            sums = sums + v * v
        inv_rms = lax.rsqrt(jnp.sum(sums, axis=1, keepdims=True) / width + EPS)
        position = lax.broadcasted_iota(jnp.int32, (ROWS, 1), 0) + i * ROWS
        share = jnp.where(position < length, inv_len, 0.0)
        weight = share * inv_rms
        cubed = weight * inv_rms * inv_rms / width
        lane = lax.broadcasted_iota(jnp.int32, (ROWS, 128), 1)
        coef_out[rows, :] = jnp.where(lane == 0, weight, cubed)
        weight_row = jnp.broadcast_to(weight, (ROWS, 128)).T[0:1, :]
        parts = jnp.dot(stack3(weight_row), x_v[rows, :], preferred_element_type=f32)
        pooled = pooled + (parts[0:1] + (parts[1:2] + parts[2:3]))
    small[1].wait()
    gain_f[...] = gain_v[...].astype(f32).reshape(1, width)
    gain = gain_f[...]
    pooled_v[...] = jnp.broadcast_to(pooled * gain, (16, width)).astype(bf16)

    raw = jnp.zeros((16, proj.shape[1]), f32)
    for i in range(n_p):
        loads[n_x + i].wait()
        cut = slice(i * PROJ, (i + 1) * PROJ)
        raw = raw + jnp.dot(pooled_v[:, cut], proj[cut, :], preferred_element_type=f32)
    raw = raw[0:8]
    magnitude = jnp.sqrt(jnp.sum(raw * raw, axis=1, keepdims=True) + EPS)
    unit = raw / magnitude
    own = unit.astype(bf16)
    mine = x * 2 + core
    kept = core * 4 + x
    for k in range(8):
        pieces[k] = own[0:1, k * 128 : (k + 1) * 128].astype(f32)

    for c in small[2:]:
        c.wait()
    pairs = target.shape[0]
    perm_row = perm_v[...].astype(f32).reshape(1, pairs)

    def prepare():
        def transpose(i, _):
            at = pl.ds(pl.multiple_of(i * 256, 256), 256)
            proj_t[:, at] = proj[at, :].T
            return 0

        lax.fori_loop(0, width // 256, transpose, 0)
        perm_col = jnp.broadcast_to(perm_row, (128, pairs)).T[:, 0:1]
        column = lax.broadcasted_iota(jnp.int32, (pairs, pairs), 1).astype(f32)
        target[...] = jnp.where(column == perm_col, 1.0, 0.0)
        xg_proj[...] = jnp.zeros_like(xg_proj)

        def gained(i, _):
            at = pl.ds(pl.multiple_of(i * PROJ, PROJ), PROJ)
            xg = x_v[:, at].astype(f32) * gain_f[:, at]
            high = xg.astype(bf16)
            low = (xg - high.astype(f32)).astype(bf16)
            both = jnp.dot(
                jnp.concatenate([high, low], axis=0), proj[at, :], preferred_element_type=f32
            )
            xg_proj[...] += both[:length_rows] + both[length_rows:]
            return 0

        lax.fori_loop(0, n_p, gained, 0)

    pl.when(z_hi == 0)(prepare)

    def copy(k, ref, d, src=None):
        out = pltpu.make_async_remote_copy(
            src_ref=ref if src is None else src, dst_ref=ref, send_sem=send_sem.at[k], recv_sem=recv_sem.at[k],
            device_id=device(d), device_id_type=MESH,
        )
        out.start()
        return out

    def sent(copies):
        for c in copies:
            c.wait_send()

    def tile(q):
        return pl.ds(pl.multiple_of(core * 512 + (q % 4) * 128, 128), 128)

    pl.semaphore_wait(barrier, len(PEERS))
    rows_in = [
        copy(i, rows8.at[mine], d, pieces.at[(core + d[3]) % 2 * 4 + (x + d[0]) % NX])
        for i, d in enumerate(XC)
    ]
    rows8[mine] = pieces[kept]
    for c in rows_in:
        c.wait_recv()
    block = emb.at[z_hi, y_far, y_par, z_lo]
    block[:, tile(x)] = rows8[...].reshape(8, 128).astype(bf16)

    cut = emb.at[z_hi, y_far, y_par, z_lo, :, tile(x)]
    far_in = [copy(AT_FAR + i, cut, d) for i, d in enumerate(FAR)]
    sent(rows_in)
    for c in far_in:
        c.wait_recv()

    near = []
    for i, (_, copies) in enumerate(MID):
        near.append([
            copy(AT_MID + 2 * i + j, emb.at[:, pl.ds(*part), y_par, z_lo, :, tile(x)], d)
            for j, (d, part) in enumerate(copies)
        ])

    held = x - 2 * y - z + 32
    classes = [(y_par, z_lo)]
    classes += [((y_par + dy) % 2, (z_lo - dz + 4) % 4) for (dy, dz), _ in MID]
    neighbours = []
    for i, (par, lo) in enumerate(classes):
        for c in near[i - 1] if i else ():
            c.wait_recv()
        base = AT_LAST + len(LAST) * (4 * par + lo)
        cols = tile(held + 2 * par + lo)
        neighbours.append([
            copy(base + j, emb.at[:, pl.ds(*part), par, lo, :, cols], d)
            for j, (d, part) in enumerate(LAST)
        ])
        if i == 0:
            sent(far_in)
    for copies in near:
        sent(copies)
    half = pl.ds(pl.multiple_of(core * 512, 512), 512)
    arriving = []
    for i, (par, lo) in enumerate(classes):
        for c in neighbours[i]:
            c.wait_recv()
        arriving.append(copy(AT_SIB + 4 * par + lo, emb.at[:, :, par, lo, :, half], SIBLING))
    for copies in neighbours:
        sent(copies)
    pl.when(z_hi != 0)(prepare)
    for c in arriving:
        c.wait_recv()

    everyone = emb[...].reshape(2 * pairs, emb.shape[-1])
    codes, docs = everyone[:pairs], everyone[pairs:]
    scores = INV_TEMP * contract_last(codes, docs)
    exps = jnp.exp(scores)
    code_totals = jnp.sum(exps, axis=1, keepdims=True)
    doc_totals = jnp.sum(exps, axis=0, keepdims=True)
    score_v[...] = scores
    code_row = jnp.broadcast_to(code_totals, (pairs, 128)).T[0:1, :]

    me = z_hi * (pairs * 2 // 3) + dp
    is_code = me < pairs
    other_totals = jnp.where(is_code, doc_totals, code_row)
    other_blocks = jnp.where(is_code, pairs // 8, 0)
    flat = emb.reshape(2 * pairs // 8, 8, emb.shape[-1])
    others = flat[pl.ds(other_blocks, pairs // 8)].reshape(pairs, emb.shape[-1])
    own_exps = jnp.exp(INV_TEMP * contract_last(own, others)[0:1, :])
    own_total = jnp.sum(own_exps, axis=1, keepdims=True)
    columns = lax.broadcasted_iota(jnp.int32, (1, pairs), 1)
    code_id = jnp.where(is_code, me, 0)
    doc_id = jnp.where(is_code, 0, me - pairs)
    code_hit = columns == jnp.full((1, 1), perm_s[code_id], jnp.int32)
    doc_hit = perm_row == jnp.full((1, 1), doc_id, jnp.int32).astype(f32)
    hit = jnp.where(is_code, jnp.where(code_hit, 1.0, 0.0), jnp.where(doc_hit, 1.0, 0.0))
    factors = own_exps / own_total + own_exps / other_totals - 2.0 * hit
    terms = jnp.dot(stack3(factors), others, preferred_element_type=f32)
    demb = (LOSS_SCALE * INV_TEMP) * (terms[0:1] + (terms[1:2] + terms[2:3]))
    unit_row = unit[0:1]
    projected = jnp.sum(unit_row * demb, axis=1, keepdims=True)
    grad_raw = (demb - unit_row * projected) / magnitude[0:1]
    grad_rows = jnp.broadcast_to(grad_raw, (16, grad_raw.shape[1])).astype(bf16)
    grad_pooled = jnp.dot(grad_rows, proj_t[...], preferred_element_type=f32)
    g_out[...] = grad_pooled[0:1] * gain_f[...]
    dots = jnp.sum(xg_proj[...] * grad_rows[0:1].astype(f32), axis=1, keepdims=True)
    lane = lax.broadcasted_iota(jnp.int32, coef_out.shape, 1)
    coef_out[...] = jnp.where(lane == 1, coef_out[...] * dots, coef_out[...])
    log_sum = jnp.sum(jnp.log(doc_totals) + jnp.log(code_row))
    loss_out[0, 0] = (log_sum - 2.0 * jnp.sum(target[...] * score_v[...])) / (2 * pairs)
    for c in arriving:
        c.wait_send()


def out_kernel(hidden, g_h, coef_h, out, x_v, g, coef, o_v, in_sem, out_sem):
    n, rows = x_v.shape[0] // OUT_ROWS, [pl.ds(i, OUT_ROWS) for i in range(0, x_v.shape[0], OUT_ROWS)]
    small = [
        pltpu.make_async_copy(g_h, g, in_sem.at[n]),
        pltpu.make_async_copy(coef_h, coef, in_sem.at[n + 1]),
    ]
    loads = [pltpu.make_async_copy(hidden.at[0, r], x_v.at[r], in_sem.at[i]) for i, r in enumerate(rows)]
    stores = [pltpu.make_async_copy(o_v.at[r], out.at[0, r], out_sem.at[i]) for i, r in enumerate(rows)]
    for c in small + loads:
        c.start()
    for c in small:
        c.wait()
    for r, load, store in zip(rows, loads, stores):
        load.wait()
        grad = coef[r, 0:1] * g[...] - x_v[r, :].astype(f32) * coef[r, 1:2]
        o_v[r, :] = grad.astype(bf16)
        store.start()
    for store in stores:
        store.wait()


def body(hidden, lengths, pair_perm, norm_gain, projection):
    _, length_rows, width = hidden.shape
    embed = projection.shape[1]
    pairs = pair_perm.shape[0]
    g, coef, loss = pl.pallas_call(
        main_kernel,
        out_shape=(
            jax.ShapeDtypeStruct((1, width), f32),
            jax.ShapeDtypeStruct((length_rows, 128), f32),
            jax.ShapeDtypeStruct((1, 1), f32),
        ),
        in_specs=[HBM] * 5,
        out_specs=(VMEM, VMEM, SMEM),
        scratch_shapes=[
            pltpu.SMEM(lengths.shape, jnp.int32),
            pltpu.SMEM(pair_perm.shape, jnp.int32),
            pltpu.VMEM(pair_perm.shape, jnp.int32),
            pltpu.VMEM((length_rows, width), bf16),
            pltpu.VMEM((width, embed), bf16),
            pltpu.VMEM((embed, width), bf16),
            pltpu.VMEM((width,), bf16),
            pltpu.VMEM((1, width), f32),
            pltpu.VMEM((8, 1, 128), f32),
            pltpu.VMEM((8, 1, 128), f32),
            pltpu.VMEM((3, 4, 2, 4, 8, embed), bf16),
            pltpu.VMEM((pairs, pairs), f32),
            pltpu.VMEM((pairs, pairs), f32),
            pltpu.VMEM((16, width), bf16),
            pltpu.VMEM((length_rows, embed), f32),
            pltpu.SemaphoreType.DMA((length_rows // ROWS + width // PROJ,)),
            pltpu.SemaphoreType.DMA((4,)),
            pltpu.SemaphoreType.DMA((N_COPIES,)),
            pltpu.SemaphoreType.DMA((N_COPIES,)),
        ],
        compiler_params=pltpu.CompilerParams(
            collective_id=0, has_side_effects=True, vmem_limit_bytes=60 << 20
        ),
        name="main",
    )(hidden, lengths, pair_perm, norm_gain, projection)
    n_out = length_rows // OUT_ROWS
    grad = pl.pallas_call(
        out_kernel,
        out_shape=jax.ShapeDtypeStruct(hidden.shape, bf16),
        in_specs=[HBM] * 3,
        out_specs=HBM,
        scratch_shapes=[
            pltpu.VMEM((length_rows, width), bf16),
            pltpu.VMEM((1, width), f32),
            pltpu.VMEM((length_rows, 128), f32),
            pltpu.VMEM((length_rows, width), bf16),
            pltpu.SemaphoreType.DMA((n_out + 2,)),
            pltpu.SemaphoreType.DMA((n_out,)),
        ],
        compiler_params=pltpu.CompilerParams(vmem_limit_bytes=60 << 20),
        name="hidden_grad",
    )(hidden, g, coef)
    return grad, loss.reshape(())


def solution(mesh):
    in_specs = (P(("section", "dp"), None, None), P(("section", "dp")), P(), P(), P())
    out_specs = (P(("section", "dp"), None, None), P())
    return jax.shard_map(body, mesh=mesh, in_specs=in_specs, out_specs=out_specs, check_vma=False)
```
